32 devices in a mesh: groups: 2 (over y), ctx: 4 (over z), dp: 2 (over x), mp: 2 (over core).
Axes of the slice: x: 2, y: 2, z: 4, core: 2. Of those that a mesh axis runs over, the one named last changes fastest.
Arguments:
- mixer_input: bfloat16 [4, 4096, 4096], P(('groups', 'dp'), 'ctx', 'mp'), parts along dimension 0, may hold values from -6 to 6
- gate_input: bfloat16 [4, 4096, 4096], P(('groups', 'dp'), 'ctx', 'mp'), parts along dimension 0, may hold values from -6 to 6
- input_proj: bfloat16 [4, 4096, 128], P(('groups', 'dp'), 'ctx'), parts along dimension 0, may hold values from -6 to 6
- output_proj: bfloat16 [4, 4096, 128], P(('groups', 'dp'), 'ctx'), parts along dimension 0, may hold values from -6 to 6
- step_raw: float32 [4, 32, 4096], P(('groups', 'dp'), 'mp', 'ctx'), parts along dimension 0, may hold values from -1 to 1
- decay_rate: float32 [32], P('mp'), may hold values from 2.4414063e-05 to 0.05
- norm_gain: float32 [4096], P('mp'), may hold values from 0.1 to 1.9
- doc_lengths: int32 [4, 16], P(('groups', 'dp')), parts along dimension 0, may hold values from 1 to 3072, 4096 in all within a row
- partner: int32 [64], P(('groups', 'dp')), parts along dimension 0, may hold values from 0 to 31, as said below
Outputs:
- mixed: bfloat16 [4, 4096, 4096], P(('groups', 'dp'), 'ctx', 'mp'), parts along dimension 0
- embedding: float32 [64, 4096], P(('groups', 'dp'), 'mp'), parts along dimension 0
- doc_loss: float32 [64], P(('groups', 'dp')), parts along dimension 0
The draws below stay inside these ranges and needn't reach their ends.
There are 2 independent parts, one for each index of `groups`. The reference program is written for one: setup_inputs(seed, part) draws one part's arguments, and reference() takes and returns one part's arrays. A program takes and returns all parts, laid end to end along the dimension named above; an argument that names none is the same for every part. Nothing has to cross between parts.
Inputs may be any that keep to these rules, and one draw needn't show every extreme that they name: `doc_lengths`: each row's lengths sum to 4096; the largest of each row is exactly 3072. partner pairs the documents: partner[partner[i]] = i and partner[i] != i.
All inputs are finite; a program needn't handle non-finite values.
Results may differ from the reference program's by a relative error of at most 0.005.
Values sent between devices are 32-bit elements; how exact they have to be, the bound alone decides.
No kernel may reach another device: no remote copies, remote signals or barrier semaphores. Data moves between devices by JAX's collectives and lax.ppermute only.
A program may use at most 128 MiB of HBM per device.

```python
import math
import jax
import jax.numpy as jnp
import numpy as np
from jax import lax

H = 32
HEAD = 128
STATE = 128
DOCS = 16
SPAN = 256
WIDTH = 4096
ROWS = 2
SEQ = 4096
LONG = 3072
ALL_DOCS = 32


def draw_decay_rate(key, part):
    key = jax.random.fold_in(key, 11)
    first, second, third = jax.random.split(key, 3)
    share = 0.5
    coin = jax.random.uniform(first, (H,), jnp.float32)
    slow_rate = jnp.exp(jnp.log(0.1 / SEQ) + jax.random.uniform(second, (H,), jnp.float32) * jnp.log(15.0))
    fast_rate = jnp.exp(jnp.log(0.02) + jax.random.uniform(third, (H,), jnp.float32) * jnp.log(2.5))
    return jnp.where(coin < share, slow_rate, fast_rate).astype(jnp.float32)


def draw_partner(key, part):
    key = jax.random.fold_in(key, 23)
    order = jax.random.permutation(key, ALL_DOCS).astype(jnp.int32)
    half = ALL_DOCS // 2
    firsts = order[:half]
    seconds = order[half:]
    paired = jnp.zeros((ALL_DOCS,), jnp.int32)
    paired = paired.at[firsts].set(seconds)
    paired = paired.at[seconds].set(firsts)
    return paired


def level_of(own_key, extent, cuts, low, top_value):
    factor_of, own = 1.0, jax.random.fold_in(own_key, 6)
    for axis_at, shards_of in cuts:
        draws = jnp.exp(jax.random.uniform(jax.random.fold_in(own, axis_at), (shards_of,), jnp.float32, low / len(cuts), top_value / len(cuts)))
        factor_of = factor_of * jnp.repeat(draws, extent[axis_at] // shards_of).reshape([-1 if axis == axis_at else 1 for axis in range(len(extent))])
    return factor_of


def length_profile(count, total, reach, lean):
    loads = [(1 << 20) // math.isqrt(standing ** lean) + 1 for standing in range(2, count + 1)]
    surplus, given = total - reach - (count - 1), [1] * (count - 1)
    while surplus > 0:
        free = [i for i in range(count - 1) if given[i] < reach]
        mass, remaining = sum([loads[i] for i in free]), surplus
        for i in free:
            more = min(reach - given[i], max(1, remaining * loads[i] // mass), surplus)
            given[i] = given[i] + more
            surplus = surplus - more
    return np.array([reach] + given)


def uneven(stream_key, number_of, total, most, slope):
    if number_of == 2:
        one = jax.random.randint(stream_key, (), max(1, total - most), min(most, total - 1) + 1)
        return jnp.stack([one, total - one])
    sizes = jnp.asarray(length_profile(number_of, total, most, slope), jnp.int32)
    couples = (number_of - 1) // 2
    donor, receiver = sizes[1:1 + 2 * couples:2], sizes[2:2 + 2 * couples:2]
    room = jnp.minimum(donor - 1, most - receiver)
    shifted = jax.random.randint(jax.random.fold_in(stream_key, 1), (couples,), 0, 1 << 20) % (room + 1)
    sizes = sizes.at[1:1 + 2 * couples:2].set(donor - shifted).at[2:2 + 2 * couples:2].set(receiver + shifted)
    return sizes[jax.random.permutation(jax.random.fold_in(stream_key, 2), number_of)]


def centred(rng, dims, width, limit, cuts=(), kind=jnp.bfloat16):
    gain = level_of(rng, dims, cuts, -0.22, 0.18) if cuts else 1.0
    array = jax.random.normal(rng, dims, jnp.float32) * width * gain
    return jnp.minimum(jnp.maximum(array, -limit), limit).astype(kind)


def setup_inputs(seed: int = 0, part: int = 0) -> dict:
    keys = jax.random.split(jax.random.key(seed), 10)
    part_splits = jax.random.split(jax.random.fold_in(keys[9], part), 10)
    return {
        "mixer_input": centred(part_splits[0], (ROWS, SEQ, WIDTH), 1.0, 6.0, ((0, 2), (1, 4), (2, 2))),
        "gate_input": centred(part_splits[1], (ROWS, SEQ, WIDTH), 1.0, 6.0, ((0, 2), (1, 4), (2, 2))),
        "input_proj": centred(part_splits[2], (ROWS, SEQ, STATE), 1.0, 6.0, ((0, 2), (1, 4))),
        "output_proj": centred(part_splits[3], (ROWS, SEQ, STATE), 1.0, 6.0, ((0, 2), (1, 4))),
        "step_raw": jnp.clip(jax.random.uniform(part_splits[4], (ROWS, H, SEQ), jnp.float32, -1.0, 1.0) * level_of(part_splits[4], (ROWS, H, SEQ), ((0, 2), (1, 2), (2, 4)), -0.4, 0.0), -1.0, 1.0),
        "decay_rate": draw_decay_rate(jax.random.fold_in(keys[9], 71), part),
        "norm_gain": jnp.clip(1.0 + 0.18 * jax.random.normal(keys[6], (WIDTH,), jnp.float32), 0.1, 1.9),
        "doc_lengths": jax.vmap(lambda own: uneven(own, DOCS, SEQ, LONG, 2))(jax.random.split(part_splits[7], ROWS)).reshape((ROWS, DOCS)).astype(jnp.int32),
        "partner": draw_partner(jax.random.fold_in(jax.random.fold_in(keys[9], part), 71), part),
    }


HIGH = lax.Precision.HIGHEST

def doc_index(places, ends):
    found = lax.optimization_barrier(jnp.sum((places[:, None] >= ends[None, :]).astype(jnp.int32), axis=1)).astype(jnp.int32)
    return jnp.where(places < 0, -1, found).astype(jnp.int32)

def one_block(state, items, norm_gain):
    xblk, zblk, bblk, cblk, sblk, lblk, dblk, prior = items
    cumlog = jnp.cumsum(lblk, axis=1)
    lower = jnp.tril(jnp.ones((SPAN, SPAN), dtype=bool))
    same = (dblk[:, None] == dblk[None, :]) & lower
    scores = jnp.einsum('is,js->ij', cblk.astype(jnp.float32), bblk.astype(jnp.float32), precision=HIGH)
    spread = cumlog[:, :, None] - cumlog[:, None, :]
    factor = jnp.where(same[None], jnp.exp(jnp.where(same[None], spread, 0.0)), 0.0)
    weights = (scores[None] * factor * sblk[:, None, :]).astype(jnp.bfloat16)
    inputs = xblk.reshape(SPAN, H, HEAD)
    intra = jnp.einsum('hij,jhp->ihp', weights.astype(jnp.float32), inputs.astype(jnp.float32), precision=HIGH)
    tail = jnp.exp(cumlog[:, -1:] - cumlog) * (dblk == dblk[-1])[None, :].astype(jnp.float32) * sblk
    carried = (inputs.astype(jnp.float32) * tail.T[:, :, None]).astype(jnp.bfloat16)
    block_state = jnp.einsum('js,jhp->hsp', bblk.astype(jnp.float32), carried.astype(jnp.float32), precision=HIGH)
    entry = jnp.exp(cumlog) * (dblk == prior)[None, :].astype(jnp.float32)
    from_state = jnp.einsum('is,hsp->ihp', cblk.astype(jnp.float32), state, precision=HIGH) * entry.T[:, :, None]
    output = intra + from_state
    block_decay = jnp.exp(cumlog[:, -1]) * (dblk[-1] == prior).astype(jnp.float32)
    new_state = block_decay[:, None, None] * state + block_state
    gated = output * jax.nn.silu(zblk.reshape(SPAN, H, HEAD).astype(jnp.float32))
    normed = gated * lax.rsqrt(lax.optimization_barrier(jnp.mean(gated * gated, axis=2, keepdims=True)) + 1e-05) * norm_gain.reshape(H, HEAD)
    return (new_state, normed.reshape(SPAN, H * HEAD).astype(jnp.bfloat16))

def mix_row(mixer_row, gate_row, in_row, out_row, step_row, lengths, decay_rate, norm_gain):
    nblocks = SEQ // SPAN
    ends = jnp.cumsum(lengths).astype(jnp.int32)
    doc_ids = doc_index(jnp.arange(SEQ, dtype=jnp.int32), ends)
    before = doc_index(jnp.arange(nblocks, dtype=jnp.int32) * SPAN - 1, ends)
    steps = jax.nn.softplus(step_row)
    logdecay = -decay_rate[:, None] * steps
    items = (mixer_row.reshape(nblocks, SPAN, H * HEAD), gate_row.reshape(nblocks, SPAN, H * HEAD), in_row.reshape(nblocks, SPAN, STATE), out_row.reshape(nblocks, SPAN, STATE), steps.reshape(H, nblocks, SPAN).transpose(1, 0, 2), logdecay.reshape(H, nblocks, SPAN).transpose(1, 0, 2), doc_ids.reshape(nblocks, SPAN), before)
    start = jnp.zeros((H, STATE, HEAD), jnp.float32)
    _, blocks = lax.scan(lambda carry, blk: one_block(carry, blk, norm_gain), start, items)
    mixed = blocks.reshape(SEQ, H * HEAD)
    member = (doc_ids[None, :] == jnp.arange(DOCS, dtype=jnp.int32)[:, None]).astype(jnp.bfloat16)
    pooled = jnp.dot(member, mixed, preferred_element_type=jnp.float32) / lengths[:, None].astype(jnp.float32)
    return (mixed, pooled)

def reference(mixer_input, gate_input, input_proj, output_proj, step_raw, decay_rate, norm_gain, doc_lengths, partner):
    mixed_rows = []
    pooled_rows = []
    for row in range(ROWS):
        mixed, pooled = mix_row(mixer_input[row], gate_input[row], input_proj[row], output_proj[row], step_raw[row], doc_lengths[row], decay_rate, norm_gain)
        mixed_rows.append(mixed)
        pooled_rows.append(pooled)
    mixed = jnp.stack(mixed_rows)
    pooled = jnp.concatenate(pooled_rows, axis=0)
    inverse = lax.rsqrt(lax.optimization_barrier(jnp.mean(pooled * pooled, axis=1)) + 1e-06)
    embedding = pooled * inverse[:, None]
    similar = jnp.dot(embedding, embedding.T, precision=HIGH) / (WIDTH * 0.05)
    ident = jnp.arange(ALL_DOCS, dtype=jnp.int32)
    others = ident[:, None] != ident[None, :]
    total = lax.optimization_barrier(jnp.sum(jnp.where(others, jnp.exp(similar), 0.0), axis=1))
    picked = lax.optimization_barrier(jnp.sum(jnp.where(ident[None, :] == partner[:, None], similar, 0.0), axis=1))
    doc_loss = jnp.log(total) - picked
    return (mixed, embedding, doc_loss)
```

```python
import functools

import jax
import jax.numpy as jnp
from jax import lax
from jax.experimental import pallas as pl
from jax.experimental.pallas import tpu as pltpu
from jax.sharding import PartitionSpec as P

SPAN = 256
WIDTH = 4096
HIGH = lax.Precision.HIGHEST

CHUNKS = 8
DELAY = 2
GROUPS = 4


def dot(a, b, dims=((1,), (0,))):
    return lax.dot_general(a, b, (dims, ((), ())), preferred_element_type=jnp.float32)


def split3(v):
    hi = v.astype(jnp.bfloat16)
    rest = v - hi.astype(jnp.float32)
    mid = rest.astype(jnp.bfloat16)
    low = (rest - mid.astype(jnp.float32)).astype(jnp.bfloat16)
    return hi, mid, low


def first_end_from(ends_ref, docs, place):
    found = jnp.int32(1 << 30)
    for k in range(docs - 1, -1, -1):
        found = jnp.where(ends_ref[k] >= place, ends_ref[k], found)
    return found


def last_end_until(ends_ref, docs, place):
    found = jnp.int32(0)
    for k in range(docs):
        found = jnp.where(ends_ref[k] <= place, ends_ref[k], found)
    return found


def state_kernel(
    docs,
    ends_ref,
    off_ref,
    x_ref,
    b_ref,
    raw_ref,
    rate_ref,
    state_ref,
    e_ref,
    f_ref,
    decay_ref,
    dend_ref,
    docid_ref,
    bt_ref,
    g_ref,
):
    tokens, heads = e_ref.shape
    blocks = tokens // SPAN
    step = pl.program_id(0)
    per = state_ref.shape[0]

    @pl.when(step == 0)
    def _():
        off = off_ref[0]
        raw = raw_ref[...]
        steps = jnp.maximum(raw, 0.0) + jnp.log1p(jnp.exp(-jnp.abs(raw)))
        steps_t = steps.T
        logdecay = -rate_ref[...] * steps_t
        row = lax.broadcasted_iota(jnp.int32, (SPAN, SPAN), 0)
        col = lax.broadcasted_iota(jnp.int32, (SPAN, SPAN), 1)
        lower = jnp.where(row >= col, 1.0, 0.0).astype(jnp.bfloat16)
        cums = []
        for b in range(blocks):
            parts = split3(logdecay[b * SPAN : (b + 1) * SPAN])
            cums.append(dot(lower, parts[0]) + (dot(lower, parts[1]) + dot(lower, parts[2])))
        later = jnp.zeros((1, heads), jnp.float32)
        for b in range(blocks - 1, -1, -1):
            later = later + cums[b][SPAN - 1 :]
            rows = pl.ds(b * SPAN, SPAN)
            f = steps_t[b * SPAN : (b + 1) * SPAN] * jnp.exp(-cums[b])
            e_ref[rows, :] = jnp.exp(cums[b])
            f_ref[rows, :] = f
            g_ref[rows, :] = f * jnp.exp(later)
        start = last_end_until(ends_ref, docs, off + tokens - 1)
        through = jnp.where(start < off, 1.0, 0.0)
        decay_ref[...] = jnp.exp(later) * through
        place = lax.broadcasted_iota(jnp.int32, (tokens, 128), 0) + off
        masked = jnp.where(place >= start, b_ref[...].astype(jnp.float32), 0.0)
        bt_ref[...] = masked.T.astype(jnp.bfloat16)
        places = lax.broadcasted_iota(jnp.int32, (1, tokens), 1) + off
        dend = jnp.full((1, tokens), 1 << 30, jnp.int32)
        docid = jnp.zeros((1, tokens), jnp.int32)
        for k in range(docs - 1, -1, -1):
            dend = jnp.where(ends_ref[k] > places, ends_ref[k], dend)
            docid = docid + (places >= ends_ref[k]).astype(jnp.int32)
        dend_ref[...] = dend
        docid_ref[...] = docid

    g = g_ref[...]
    lane = lax.broadcasted_iota(jnp.int32, (1, heads), 1)
    scaled = []
    for h in range(per):
        column = jnp.sum(jnp.where(lane == step * per + h, g, 0.0), axis=1, keepdims=True)
        scaled.append((x_ref[:, h * 128 : (h + 1) * 128].astype(jnp.float32) * column).astype(jnp.bfloat16))
    total = dot(bt_ref[...], jnp.concatenate(scaled, axis=1))
    for h in range(per):
        state_ref[h] = total[:, h * 128 : (h + 1) * 128]


def finish_kernel(
    docs,
    group,
    ends_ref,
    off_ref,
    x_ref,
    z_ref,
    b_ref,
    c_ref,
    e_ref,
    f_ref,
    dend_ref,
    docid_ref,
    gain_ref,
    *rest,
):
    in_refs = rest[: CHUNKS // GROUPS]
    mixed_ref, sums_ref, right_ref, state_ref = rest[-4:]
    block = pl.program_id(0)
    per = x_ref.shape[1] // 128
    start = off_ref[0] + block * SPAN
    prior_end = jnp.where(start > 0, first_end_from(ends_ref, docs, start), 0)
    last_start = last_end_until(ends_ref, docs, start + SPAN - 1)
    each = per // len(in_refs)

    @pl.when(block == 0)
    def _():
        for h in range(per):
            state_ref[:, h * 128 : (h + 1) * 128] = in_refs[h // each][h % each]
        sums_ref[...] = jnp.zeros_like(sums_ref)

    row = lax.broadcasted_iota(jnp.int32, (SPAN, SPAN), 0)
    col = lax.broadcasted_iota(jnp.int32, (SPAN, SPAN), 1)
    same = (row >= col) & (row + start < dend_ref[...])
    scores = jnp.where(same, dot(c_ref[...], b_ref[...], ((1,), (1,))), 0.0).astype(jnp.bfloat16)
    place = lax.broadcasted_iota(jnp.int32, (SPAN, 128), 0) + start
    reach = jnp.where(place < prior_end, c_ref[...].astype(jnp.float32), 0.0).astype(jnp.bfloat16)
    tail = jnp.where(place >= last_start, b_ref[...].astype(jnp.float32), 0.0).astype(jnp.bfloat16)
    state = state_ref[...]
    high = state.astype(jnp.bfloat16)
    right_ref[SPAN : SPAN + 128] = high
    right_ref[SPAN + 128 :] = (state - high.astype(jnp.float32)).astype(jnp.bfloat16)
    for h in range(per):
        cols = slice(h * 128, (h + 1) * 128)
        head = group * per + h
        right_ref[0:SPAN, cols] = (
            x_ref[:, cols].astype(jnp.float32) * f_ref[:, head : head + 1]
        ).astype(jnp.bfloat16)
    left = jnp.concatenate([scores, reach, reach], axis=1)
    inner = dot(left, right_ref[...])
    added = dot(tail, right_ref[0:SPAN], ((0,), (0,)))
    keep = jnp.where(last_start < start, 1.0, 0.0)
    ones = jnp.full((128, 128), 1.0, jnp.bfloat16)
    for h in range(per):
        cols = slice(h * 128, (h + 1) * 128)
        head = group * per + h
        z = z_ref[:, cols].astype(jnp.float32)
        half = 0.5 * z
        e = e_ref[:, head : head + 1]
        gated = (inner[:, cols] * e) * (half + half * jnp.tanh(half))
        squares = dot((gated * gated).astype(jnp.bfloat16), ones)
        normed = gated * lax.rsqrt(squares * (1.0 / 128) + 1e-05) * gain_ref[:, cols]
        mixed_ref[:, cols] = normed.astype(jnp.bfloat16)
        state_ref[:, cols] = e[SPAN - 1 :] * (keep * state[:, cols] + added[:, cols])
    member = (
        docid_ref[...] == lax.broadcasted_iota(jnp.int32, (docs, SPAN), 0)
    ).astype(jnp.float32).astype(jnp.bfloat16)
    sums_ref[...] += dot(member, mixed_ref[...])


def on_device(
    mixer_input,
    gate_input,
    input_proj,
    output_proj,
    step_raw,
    decay_rate,
    norm_gain,
    doc_lengths,
    partner,
):
    tokens = mixer_input.shape[1]
    width = mixer_input.shape[2]
    heads = decay_rate.shape[0]
    docs = doc_lengths.shape[1]
    blocks = tokens // SPAN
    count = lax.axis_size("ctx")
    here = lax.axis_index("ctx")
    x, z = mixer_input[0], gate_input[0]
    lengths = doc_lengths[0]
    ends = jnp.cumsum(lengths).astype(jnp.int32)
    off = (here * tokens).astype(jnp.int32).reshape(1)
    per = heads // CHUNKS
    smem = pl.BlockSpec(memory_space=pltpu.SMEM)
    whole = lambda shape: pl.BlockSpec(shape, lambda i: (0,) * len(shape))
    f32 = jnp.float32
    state, e, f, decay, dend, docid = pl.pallas_call(
        functools.partial(state_kernel, docs),
        grid=(CHUNKS,),
        in_specs=[
            smem,
            smem,
            pl.BlockSpec((tokens, per * 128), lambda i: (0, i)),
            whole((tokens, 128)),
            whole((heads, tokens)),
            whole((1, heads)),
        ],
        out_specs=[
            pl.BlockSpec((per, 128, 128), lambda i: (i, 0, 0)),
            whole((tokens, heads)),
            whole((tokens, heads)),
            whole((1, heads)),
            whole((1, tokens)),
            whole((1, tokens)),
        ],
        out_shape=[
            jax.ShapeDtypeStruct((heads, 128, 128), f32),
            jax.ShapeDtypeStruct((tokens, heads), f32),
            jax.ShapeDtypeStruct((tokens, heads), f32),
            jax.ShapeDtypeStruct((1, heads), f32),
            jax.ShapeDtypeStruct((1, tokens), jnp.int32),
            jax.ShapeDtypeStruct((1, tokens), jnp.int32),
        ],
        scratch_shapes=[pltpu.VMEM((128, tokens), jnp.bfloat16), pltpu.VMEM((tokens, heads), f32)],
        compiler_params=pltpu.CompilerParams(vmem_limit_bytes=32 << 20),
        cost_estimate=pl.CostEstimate(flops=2 * tokens * 128 * width, bytes_accessed=6 << 20, transcendentals=0),
        name="states",
    )(ends, off, x, input_proj[0], step_raw[0], decay_rate.reshape(1, heads))

    pairs = [(i, (i + 1) % count) for i in range(count)]
    got = []
    for r in range(CHUNKS + DELAY * (count - 2)):
        at = jnp.clip(r - DELAY * here, 0, CHUNKS - 1) * per
        sent = lax.dynamic_slice_in_dim(state, at, per, 0)
        if r >= DELAY:
            rate = lax.dynamic_slice_in_dim(decay[0], at, per, 0)
            sent = sent + rate[:, None, None] * jnp.where(here == 0, 0.0, got[r - DELAY])
        got.append(lax.ppermute(sent, "ctx", pairs))

    def arrived(c):
        value = jnp.zeros((per, 128, 128), f32)
        for k in range(1, count):
            value = jnp.where(here == k, got[c + DELAY * (k - 1)], value)
        return value

    cols = width // GROUPS
    each = CHUNKS // GROUPS
    mixed = None
    sums = []
    for q in range(GROUPS):
        incoming = [arrived(q * each + i) for i in range(each)]
        operands = [ends, off, x, z, input_proj[0], output_proj[0], e, f, dend, docid, norm_gain.reshape(1, width)]
        specs = [
            smem,
            smem,
            pl.BlockSpec((SPAN, cols), lambda i, q=q: (i, q)),
            pl.BlockSpec((SPAN, cols), lambda i, q=q: (i, q)),
            pl.BlockSpec((SPAN, 128), lambda i: (i, 0)),
            pl.BlockSpec((SPAN, 128), lambda i: (i, 0)),
            pl.BlockSpec((SPAN, heads), lambda i: (i, 0)),
            pl.BlockSpec((SPAN, heads), lambda i: (i, 0)),
            pl.BlockSpec((1, SPAN), lambda i: (0, i)),
            pl.BlockSpec((1, SPAN), lambda i: (0, i)),
            pl.BlockSpec((1, cols), lambda i, q=q: (0, q)),
        ] + [whole((per, 128, 128))] * each
        operands += incoming
        aliases = {}
        if mixed is not None:
            aliases = {len(operands): 0}
            operands.append(mixed)
            specs.append(pl.BlockSpec(memory_space=pl.ANY))
        mixed, part = pl.pallas_call(
            functools.partial(finish_kernel, docs, q),
            grid=(blocks,),
            in_specs=specs,
            out_specs=[
                pl.BlockSpec((SPAN, cols), lambda i, q=q: (i, q)),
                whole((docs, cols)),
            ],
            out_shape=[
                jax.ShapeDtypeStruct((tokens, width), jnp.bfloat16),
                jax.ShapeDtypeStruct((docs, cols), f32),
            ],
            scratch_shapes=[pltpu.VMEM((SPAN + 256, cols), jnp.bfloat16), pltpu.VMEM((128, cols), f32)],
            input_output_aliases=aliases,
            compiler_params=pltpu.CompilerParams(vmem_limit_bytes=32 << 20),
            cost_estimate=pl.CostEstimate(
                flops=2 * tokens * cols * 1024, bytes_accessed=3 * tokens * cols * 2, transcendentals=2 * tokens * cols
            ),
            name=f"finish{q}",
        )(*operands)
        sums.append(part)

    totals = jnp.concatenate(sums, axis=1)
    reach = 1
    while reach < count:
        totals = totals + lax.ppermute(totals, "ctx", [(i, i ^ reach) for i in range(count)])
        reach *= 2
    pooled = totals / lengths[:, None].astype(f32)
    pooled_all = lax.all_gather(pooled, "dp", axis=0, tiled=True)
    part_dots = jnp.dot(pooled, pooled_all.T, precision=HIGH)
    part_squares = jnp.sum(pooled_all * pooled_all, axis=1)
    dots, squares = lax.psum((part_dots, part_squares), "mp")
    inverse_all = lax.rsqrt(squares / WIDTH + 1e-06)
    first_doc = lax.axis_index("dp") * docs
    inverse_mine = lax.dynamic_slice_in_dim(inverse_all, first_doc, docs)
    embedding = pooled * inverse_mine[:, None]
    similar = dots * inverse_mine[:, None] * inverse_all[None, :] / (WIDTH * 0.05)
    every_doc = jnp.arange(pooled_all.shape[0], dtype=jnp.int32)
    my_docs = first_doc + jnp.arange(docs, dtype=jnp.int32)
    others = every_doc[None, :] != my_docs[:, None]
    total = jnp.sum(jnp.where(others, jnp.exp(similar), 0.0), axis=1)
    picked = jnp.sum(jnp.where(every_doc[None, :] == partner[:, None], similar, 0.0), axis=1)
    doc_loss = jnp.log(total) - picked
    return (mixed[None], embedding, doc_loss)


def solution(mesh):
    in_specs = (
        P(("groups", "dp"), "ctx", "mp"),
        P(("groups", "dp"), "ctx", "mp"),
        P(("groups", "dp"), "ctx", None),
        P(("groups", "dp"), "ctx", None),
        P(("groups", "dp"), "mp", "ctx"),
        P("mp"),
        P("mp"),
        P(("groups", "dp"), None),
        P(("groups", "dp")),
    )
    out_specs = (P(("groups", "dp"), "ctx", "mp"), P(("groups", "dp"), "mp"), P(("groups", "dp")))
    return jax.shard_map(
        on_device, mesh=mesh, in_specs=in_specs, out_specs=out_specs, check_vma=False
    )
```

```python
import functools

import jax
import jax.numpy as jnp
from jax import lax
from jax.experimental import pallas as pl
from jax.experimental.pallas import tpu as pltpu
from jax.sharding import PartitionSpec as P

SPAN = 256
WIDTH = 4096
HIGH = lax.Precision.HIGHEST

CHUNKS = 8
DELAY = 2
VMEM = 8 << 20
STEPS = 1


def dot(a, b, dims=((1,), (0,))):
    return lax.dot_general(a, b, (dims, ((), ())), preferred_element_type=jnp.float32)


def split3(v):
    hi = v.astype(jnp.bfloat16)
    rest = v - hi.astype(jnp.float32)
    mid = rest.astype(jnp.bfloat16)
    low = (rest - mid.astype(jnp.float32)).astype(jnp.bfloat16)
    return hi, mid, low


def first_end_from(ends, place):
    found = jnp.int32(1 << 30)
    for end in reversed(ends):
        found = jnp.where(end >= place, end, found)
    return found


def last_end_until(ends, place):
    found = jnp.int32(0)
    for end in ends:
        found = jnp.where(end <= place, end, found)
    return found


def prepare_kernel(
    lengths_ref,
    off_ref,
    b_ref,
    c_ref,
    raw_ref,
    rate_ref,
    e_ref,
    f_ref,
    last_ref,
    keep_ref,
    before_ref,
    rates_ref,
    left_ref,
    tail_ref,
    far_ref,
    member_ref,
    decay_ref,
):
    tokens, heads = e_ref.shape
    blocks = tokens // SPAN
    off = off_ref[0]
    docs = member_ref.shape[0]
    ends = [lengths_ref[0, 0]]
    for k in range(1, docs):
        ends.append(ends[-1] + lengths_ref[0, k])
    raw = raw_ref[...]
    steps = (jnp.maximum(raw, 0.0) + jnp.log1p(jnp.exp(-jnp.abs(raw)))).T
    logdecay = -rate_ref[...] * steps
    row = lax.broadcasted_iota(jnp.int32, (SPAN, SPAN), 0)
    col = lax.broadcasted_iota(jnp.int32, (SPAN, SPAN), 1)
    lower = jnp.where(row >= col, 1.0, 0.0).astype(jnp.bfloat16)
    places = lax.broadcasted_iota(jnp.int32, (1, tokens), 1) + off
    dend = jnp.full((1, tokens), 1 << 30, jnp.int32)
    docid = jnp.zeros((1, tokens), jnp.int32)
    for k in range(docs - 1, -1, -1):
        dend = jnp.where(ends[k] > places, ends[k], dend)
        docid = docid + (places >= ends[k]).astype(jnp.int32)
    member_ref[...] = (
        (docid == lax.broadcasted_iota(jnp.int32, (docs, tokens), 0)).astype(jnp.float32).astype(jnp.bfloat16)
    )
    device_end = jnp.where(off > 0, first_end_from(ends, off), 0)
    so_far = jnp.zeros((1, heads), jnp.float32)
    for b in range(blocks):
        rows = slice(b * SPAN, (b + 1) * SPAN)
        parts = split3(logdecay[rows])
        cum = dot(lower, parts[0]) + (dot(lower, parts[1]) + dot(lower, parts[2]))
        e_ref[rows, :] = jnp.exp(cum)
        f_ref[rows, :] = steps[rows] * jnp.exp(-cum)
        whole = cum[SPAN - 1 :]
        start = off + b * SPAN
        last_start = last_end_until(ends, start + SPAN - 1)
        prior_end = jnp.where(start > 0, first_end_from(ends, start), 0)
        before_ref[b : b + 1, :] = jnp.exp(so_far)
        so_far = so_far + whole
        last_ref[b : b + 1, :] = jnp.exp(whole)
        keep_ref[b : b + 1, :] = jnp.exp(whole) * jnp.where(last_start < start, 1.0, 0.0)
        bb, cc = b_ref[rows, :], c_ref[rows, :]
        same = (row >= col) & (row + start < dend[:, rows])
        left_ref[rows, 0:SPAN] = jnp.where(same, dot(cc, bb, ((1,), (1,))), 0.0).astype(jnp.bfloat16)
        place = lax.broadcasted_iota(jnp.int32, (SPAN, 128), 0) + start
        cf = cc.astype(jnp.float32)
        reach = jnp.where(place < prior_end, cf, 0.0).astype(jnp.bfloat16)
        left_ref[rows, SPAN : SPAN + 128] = reach
        left_ref[rows, SPAN + 128 :] = reach
        far_ref[rows, :] = jnp.where(place < device_end, cf, 0.0).astype(jnp.bfloat16)
        masked = jnp.where(place >= last_start, bb.astype(jnp.float32), 0.0)
        tail_ref[b * 128 : (b + 1) * 128, :] = masked.T.astype(jnp.bfloat16)
    through = jnp.where(last_end_until(ends, off + tokens - 1) < off, 1.0, 0.0)
    decay_ref[...] = jnp.broadcast_to(jnp.exp(so_far) * through, (128, heads)).T
    here = off // tokens
    per = heads // CHUNKS
    for r in range(rates_ref.shape[0] // per):
        chunk = jnp.clip(r - DELAY * here, 0, CHUNKS - 1)
        for h in range(per):
            rates_ref[r * per + h : r * per + h + 1, :] = decay_ref[pl.ds(chunk * per + h, 1), :]


def local_kernel(
    first,
    x_ref,
    z_ref,
    e_ref,
    f_ref,
    left_ref,
    tail_ref,
    last_ref,
    keep_ref,
    before_ref,
    local_ref,
    gate_ref,
    out_ref,
    right_ref,
    state_ref,
):
    block = pl.program_id(0)
    per = x_ref.shape[1] // 128

    @pl.when(block == 0)
    def _():
        state_ref[...] = jnp.zeros_like(state_ref)

    state = state_ref[...]
    high = state.astype(jnp.bfloat16)
    right_ref[SPAN : SPAN + 128] = high
    right_ref[SPAN + 128 :] = (state - high.astype(jnp.float32)).astype(jnp.bfloat16)
    for h in range(per):
        cols = slice(h * 128, (h + 1) * 128)
        head = first + h
        right_ref[0:SPAN, cols] = (
            x_ref[:, cols].astype(jnp.float32) * f_ref[:, head : head + 1]
        ).astype(jnp.bfloat16)
    inner = dot(left_ref[...], right_ref[...])
    added = dot(tail_ref[...], right_ref[0:SPAN])
    for h in range(per):
        cols = slice(h * 128, (h + 1) * 128)
        head = first + h
        half = 0.5 * z_ref[:, cols].astype(jnp.float32)
        gate = (half + half * jnp.tanh(half)) * e_ref[:, head : head + 1]
        gate_ref[:, cols] = (gate * before_ref[pl.ds(block, 1), head : head + 1]).astype(jnp.bfloat16)
        local_ref[:, cols] = inner[:, cols] * gate
        new = (
            keep_ref[pl.ds(block, 1), head : head + 1] * state[:, cols]
            + last_ref[pl.ds(block, 1), head : head + 1] * added[:, cols]
        )
        state_ref[:, cols] = new
        out_ref[h] = new


def finish_kernel(
    local_ref,
    gate_ref,
    far_ref,
    in_ref,
    gain_ref,
    member_ref,
    *rest,
):
    mixed_ref, sums_ref = rest[-2:]
    step = pl.program_id(0)
    cols = local_ref.shape[1]
    per = cols // 128
    row = lax.broadcasted_iota(jnp.int32, (cols, cols), 0)
    col = lax.broadcasted_iota(jnp.int32, (cols, cols), 1)
    mean = jnp.where(row // 128 == col // 128, 1.0 / 128, 0.0).astype(jnp.bfloat16)
    state = jnp.concatenate([in_ref[h] for h in range(per)], axis=1)
    high = state.astype(jnp.bfloat16)
    low = (state - high.astype(jnp.float32)).astype(jnp.bfloat16)
    right = jnp.concatenate([high, low], axis=0)
    gain = gain_ref[...]
    for b in range(local_ref.shape[0] // SPAN):
        rows = slice(b * SPAN, (b + 1) * SPAN)
        far = far_ref[rows, :]
        remote = dot(jnp.concatenate([far, far], axis=1), right)
        gated = local_ref[rows, :] + gate_ref[rows, :].astype(jnp.float32) * remote
        squares = dot((gated * gated).astype(jnp.bfloat16), mean)
        mixed_ref[rows, :] = (gated * lax.rsqrt(squares + 1e-05) * gain).astype(jnp.bfloat16)
    found = dot(member_ref[...], mixed_ref[...])

    @pl.when(step == 0)
    def _():
        sums_ref[...] = found

    @pl.when(step > 0)
    def _():
        sums_ref[...] += found


def after(value, *others):
    return lax.optimization_barrier((value, *others))[0]


def swapped(value, axis, by):
    return lax.ppermute(value, axis, [(i, i ^ by) for i in range(lax.axis_size(axis))])


def on_device(
    mixer_input,
    gate_input,
    input_proj,
    output_proj,
    step_raw,
    decay_rate,
    norm_gain,
    doc_lengths,
    partner,
):
    tokens = mixer_input.shape[1]
    width = mixer_input.shape[2]
    heads = decay_rate.shape[0]
    docs = doc_lengths.shape[1]
    blocks = tokens // SPAN
    count = lax.axis_size("ctx")
    here = lax.axis_index("ctx")
    x, z = mixer_input[0], gate_input[0]
    lengths = doc_lengths[0]
    row = lax.axis_index("dp")
    off = here * tokens
    places = [here == k for k in range(count)]
    firsts = [(row ^ j) * docs for j in range(lax.axis_size("dp"))]
    off, *rest = lax.optimization_barrier((off, *places, *firsts))
    places, firsts = rest[:count], rest[count:]
    off = off.astype(jnp.int32).reshape(1)
    per = heads // CHUNKS
    rounds = CHUNKS + DELAY * (count - 2)
    cols = per * 128
    f32, bf16 = jnp.float32, jnp.bfloat16
    smem = pl.BlockSpec(memory_space=pltpu.SMEM)
    whole = lambda *shape: pl.BlockSpec(shape, lambda *i: (0,) * len(shape))
    rows = lambda *shape: pl.BlockSpec(shape, lambda i: (i, 0))
    array = jax.ShapeDtypeStruct
    limit = pltpu.CompilerParams(vmem_limit_bytes=VMEM)

    shapes = [
        array((tokens, heads), f32),
        array((tokens, heads), f32),
        array((blocks, heads), f32),
        array((blocks, heads), f32),
        array((blocks, heads), f32),
        array((rounds * per, 128), f32),
        array((tokens, SPAN + 256), bf16),
        array((blocks * 128, SPAN), bf16),
        array((tokens, 128), bf16),
        array((docs, tokens), bf16),
    ]
    e, f, last, keep, before, rates, left, tails, far, member = pl.pallas_call(
        prepare_kernel,
        grid=(1,),
        in_specs=[smem, smem, whole(tokens, 128), whole(tokens, 128), whole(heads, tokens), whole(1, heads)],
        out_specs=[whole(*s.shape) for s in shapes],
        scratch_shapes=[pltpu.VMEM((heads, 128), f32)],
        out_shape=shapes,
        compiler_params=limit,
        cost_estimate=pl.CostEstimate(flops=1 << 28, bytes_accessed=4 << 20, transcendentals=0),
        name="prepare",
    )(doc_lengths, off, input_proj[0], output_proj[0], step_raw[0], decay_rate.reshape(1, heads))

    def local(c, last):
        block = pl.BlockSpec((SPAN, cols), lambda i: (i, c))
        return pl.pallas_call(
            functools.partial(local_kernel, c * per),
            grid=(blocks,),
            in_specs=[
                block,
                block,
                rows(SPAN, heads),
                rows(SPAN, heads),
                rows(SPAN, SPAN + 256),
                rows(128, SPAN),
                whole(blocks, heads),
                whole(blocks, heads),
                whole(blocks, heads),
            ],
            out_specs=[rows(SPAN, cols), rows(SPAN, cols), whole(per, 128, 128)],
            out_shape=[array((tokens, cols), f32), array((tokens, cols), bf16), array((per, 128, 128), f32)],
            scratch_shapes=[pltpu.VMEM((SPAN + 256, cols), bf16), pltpu.VMEM((128, cols), f32)],
            compiler_params=limit,
            cost_estimate=pl.CostEstimate(flops=1 << 20, bytes_accessed=1 << 16, transcendentals=0),
            name=f"local{c}",
        )(x, z, e, f, left, tails, last, keep, before)

    def finish(c, incoming, mixed):
        operands = [locals_[c], gates[c], far, incoming, norm_gain.reshape(1, width), member]
        specs = [
            rows(tokens // STEPS, cols),
            rows(tokens // STEPS, cols),
            rows(tokens // STEPS, 128),
            whole(per, 128, 128),
            pl.BlockSpec((1, cols), lambda i: (0, c)),
            pl.BlockSpec((docs, tokens // STEPS), lambda i: (0, i)),
        ]
        aliases = {}
        if mixed is not None:
            aliases = {len(operands): 0}
            operands.append(mixed)
            specs.append(pl.BlockSpec(memory_space=pl.ANY))
        return pl.pallas_call(
            finish_kernel,
            grid=(STEPS,),
            in_specs=specs,
            out_specs=[pl.BlockSpec((tokens // STEPS, cols), lambda i: (i, c)), whole(docs, cols)],
            out_shape=[array((tokens, width), bf16), array((docs, cols), f32)],
            input_output_aliases=aliases,
            compiler_params=limit,
            cost_estimate=pl.CostEstimate(flops=1 << 20, bytes_accessed=1 << 16, transcendentals=0),
            name=f"finish{c}",
        )(*operands)

    pairs = [(i, (i + 1) % count) for i in range(count)]
    locals_, gates, states, got, sums = [], [], [], [], []
    mixed = None
    sent = None

    def arrived(c, *ready):
        found = [got[c + DELAY * k] for k in range(count - 1)]
        found = lax.optimization_barrier((*found, *ready))
        value = jnp.zeros((per, 128, 128), f32)
        for k in range(1, count):
            value = jnp.where(places[k], found[k - 1], value)
        return value

    for r in range(rounds):
        ready = [] if sent is None else [sent]
        if r < CHUNKS:
            part, gate, state = local(r, after(last, *ready))
            locals_.append(part)
            gates.append(gate)
            states.append(state)
            ready.append(state)
        old = r - 1 - DELAY - DELAY * (count - 2)
        if old >= 0:
            mixed, part = finish(old, arrived(old, sent), mixed)
            sums.append(part)
            ready.append(part)
        mine = states[min(r, CHUNKS - 1)]
        for k in range(1, count):
            c = r - DELAY * k
            if 0 <= c < CHUNKS:
                mine = jnp.where(places[k], states[c], mine)
        if r >= DELAY:
            arriving = after(got[r - DELAY], *ready)
            mine = mine + rates[r * per : (r + 1) * per, None] * jnp.where(places[0], 0.0, arriving)
        elif r > 0:
            mine = after(mine, *ready)
        sent = mine
        got.append(lax.ppermute(sent, "ctx", pairs))
    for c in range(len(sums), CHUNKS):
        mixed, part = finish(c, arrived(c, *sums[-1:]), mixed)
        sums.append(part)

    totals = jnp.concatenate(sums, axis=1)
    if count <= 4:
        parts = [swapped(totals, "ctx", j) for j in range(1, count)]
        for part in parts:
            totals = totals + part
    else:
        reach = 1
        while reach < count:
            totals = totals + swapped(totals, "ctx", reach)
            reach *= 2
    pooled = totals / lengths[:, None].astype(f32)
    every = [pooled] + [swapped(pooled, "dp", j) for j in range(1, lax.axis_size("dp"))]
    found = [jnp.dot(pooled, one.T, precision=HIGH) for one in every]
    found += [jnp.sum(one * one, axis=1)[None] for one in every]
    found = jnp.concatenate(found, axis=0)
    for j in range(1, lax.axis_size("mp")):
        found = found + swapped(found, "mp", j)
    own = lax.rsqrt(found[len(every) * docs] / WIDTH + 1e-06)
    embedding = pooled * own[:, None]
    total = jnp.zeros((docs,), f32)
    picked = jnp.zeros((docs,), f32)
    ids = jnp.arange(docs, dtype=jnp.int32)
    for j in range(len(every)):
        other = lax.rsqrt(found[len(every) * docs + j] / WIDTH + 1e-06)
        similar = found[j * docs : (j + 1) * docs] * own[:, None] * other[None, :] / (WIDTH * 0.05)
        theirs = firsts[j] + ids
        others = theirs[None, :] != (firsts[0] + ids)[:, None]
        total = total + jnp.sum(jnp.where(others, jnp.exp(similar), 0.0), axis=1)
        picked = picked + jnp.sum(jnp.where(theirs[None, :] == partner[:, None], similar, 0.0), axis=1)
    doc_loss = jnp.log(total) - picked
    return (mixed[None], embedding, doc_loss)


def solution(mesh):
    in_specs = (
        P(("groups", "dp"), "ctx", "mp"),
        P(("groups", "dp"), "ctx", "mp"),
        P(("groups", "dp"), "ctx", None),
        P(("groups", "dp"), "ctx", None),
        P(("groups", "dp"), "mp", "ctx"),
        P("mp"),
        P("mp"),
        P(("groups", "dp"), None),
        P(("groups", "dp")),
    )
    out_specs = (P(("groups", "dp"), "ctx", "mp"), P(("groups", "dp"), "mp"), P(("groups", "dp")))
    return jax.shard_map(
        on_device, mesh=mesh, in_specs=in_specs, out_specs=out_specs, check_vma=False
    )
```

```python
import functools

import jax
import jax.numpy as jnp
from jax import lax
from jax.experimental import pallas as pl
from jax.experimental.pallas import tpu as pltpu
from jax.sharding import PartitionSpec as P

SPAN = 256
WIDTH = 4096
HIGH = lax.Precision.HIGHEST

CHUNKS = 8
DELAY = 3
VMEM = 8 << 20
BATCHES = (8,)


def dot(a, b, dims=((1,), (0,))):
    return lax.dot_general(a, b, (dims, ((), ())), preferred_element_type=jnp.float32)


def split3(v):
    hi = v.astype(jnp.bfloat16)
    rest = v - hi.astype(jnp.float32)
    mid = rest.astype(jnp.bfloat16)
    low = (rest - mid.astype(jnp.float32)).astype(jnp.bfloat16)
    return hi, mid, low


def first_end_from(ends, place):
    found = jnp.int32(1 << 30)
    for end in reversed(ends):
        found = jnp.where(end >= place, end, found)
    return found


def last_end_until(ends, place):
    found = jnp.int32(0)
    for end in ends:
        found = jnp.where(end <= place, end, found)
    return found


def prepare_kernel(
    lengths_ref,
    off_ref,
    b_ref,
    c_ref,
    raw_ref,
    rate_ref,
    e_ref,
    f_ref,
    last_ref,
    keep_ref,
    before_ref,
    rates_ref,
    left_ref,
    tail_ref,
    far_ref,
    member_ref,
    decay_ref,
):
    tokens, heads = e_ref.shape
    blocks = tokens // SPAN
    off = off_ref[0]
    docs = member_ref.shape[0]
    ends = [lengths_ref[0, 0]]
    for k in range(1, docs):
        ends.append(ends[-1] + lengths_ref[0, k])
    raw = raw_ref[...]
    steps = (jnp.maximum(raw, 0.0) + jnp.log1p(jnp.exp(-jnp.abs(raw)))).T
    logdecay = -rate_ref[...] * steps
    row = lax.broadcasted_iota(jnp.int32, (SPAN, SPAN), 0)
    col = lax.broadcasted_iota(jnp.int32, (SPAN, SPAN), 1)
    lower = jnp.where(row >= col, 1.0, 0.0).astype(jnp.bfloat16)
    places = lax.broadcasted_iota(jnp.int32, (1, tokens), 1) + off
    dend = jnp.full((1, tokens), 1 << 30, jnp.int32)
    docid = jnp.zeros((1, tokens), jnp.int32)
    for k in range(docs - 1, -1, -1):
        dend = jnp.where(ends[k] > places, ends[k], dend)
        docid = docid + (places >= ends[k]).astype(jnp.int32)
    member_ref[...] = (
        (docid == lax.broadcasted_iota(jnp.int32, (docs, tokens), 0)).astype(jnp.float32).astype(jnp.bfloat16)
    )
    device_end = jnp.where(off > 0, first_end_from(ends, off), 0)
    so_far = jnp.zeros((1, heads), jnp.float32)
    for b in range(blocks):
        rows = slice(b * SPAN, (b + 1) * SPAN)
        parts = split3(logdecay[rows])
        cum = dot(lower, parts[0]) + (dot(lower, parts[1]) + dot(lower, parts[2]))
        e_ref[rows, :] = jnp.exp(cum)
        f_ref[rows, :] = steps[rows] * jnp.exp(-cum)
        whole = cum[SPAN - 1 :]
        start = off + b * SPAN
        last_start = last_end_until(ends, start + SPAN - 1)
        prior_end = jnp.where(start > 0, first_end_from(ends, start), 0)
        before_ref[b : b + 1, :] = jnp.exp(so_far)
        so_far = so_far + whole
        last_ref[b : b + 1, :] = jnp.exp(whole)
        keep_ref[b : b + 1, :] = jnp.exp(whole) * jnp.where(last_start < start, 1.0, 0.0)
        bb, cc = b_ref[rows, :], c_ref[rows, :]
        same = (row >= col) & (row + start < dend[:, rows])
        left_ref[rows, 0:SPAN] = jnp.where(same, dot(cc, bb, ((1,), (1,))), 0.0).astype(jnp.bfloat16)
        place = lax.broadcasted_iota(jnp.int32, (SPAN, 128), 0) + start
        cf = cc.astype(jnp.float32)
        reach = jnp.where(place < prior_end, cf, 0.0).astype(jnp.bfloat16)
        left_ref[rows, SPAN : SPAN + 128] = reach
        left_ref[rows, SPAN + 128 :] = reach
        far_ref[rows, :] = jnp.where(place < device_end, cf, 0.0).astype(jnp.bfloat16)
        masked = jnp.where(place >= last_start, bb.astype(jnp.float32), 0.0)
        tail_ref[b * 128 : (b + 1) * 128, :] = masked.T.astype(jnp.bfloat16)
    through = jnp.where(last_end_until(ends, off + tokens - 1) < off, 1.0, 0.0)
    decay_ref[...] = jnp.broadcast_to(jnp.exp(so_far) * through, (128, heads)).T
    here = off // tokens
    per = heads // CHUNKS
    for r in range(rates_ref.shape[0] // per):
        chunk = jnp.clip(r - DELAY * here, 0, CHUNKS - 1)
        for h in range(per):
            rates_ref[r * per + h : r * per + h + 1, :] = decay_ref[pl.ds(chunk * per + h, 1), :]


def local_kernel(
    first,
    x_ref,
    z_ref,
    e_ref,
    f_ref,
    left_ref,
    tail_ref,
    last_ref,
    keep_ref,
    before_ref,
    local_ref,
    gate_ref,
    out_ref,
):
    tokens, cols = local_ref.shape
    heads = range(first // 128, (first + cols) // 128)
    lanes = pl.ds(first, cols)

    def spread(ref, rows, count):
        return jnp.concatenate([jnp.broadcast_to(ref[rows, h : h + 1], (count, 128)) for h in heads], axis=1)

    state = None
    for b in range(tokens // SPAN):
        rows = slice(b * SPAN, (b + 1) * SPAN)
        one = slice(b, b + 1)
        scaled = (x_ref[rows, lanes].astype(jnp.float32) * spread(f_ref, rows, SPAN)).astype(jnp.bfloat16)
        added = dot(tail_ref[b * 128 : (b + 1) * 128, :], scaled)
        inner = dot(left_ref[rows, 0:SPAN], scaled)
        if state is not None:
            high = state.astype(jnp.bfloat16)
            low = (state - high.astype(jnp.float32)).astype(jnp.bfloat16)
            inner = inner + dot(left_ref[rows, SPAN:], jnp.concatenate([high, low], axis=0))
        half = 0.5 * z_ref[rows, lanes].astype(jnp.float32)
        gate = (half + half * jnp.tanh(half)) * spread(e_ref, rows, SPAN)
        local_ref[rows, :] = inner * gate
        if b > 0:
            gate = gate * spread(before_ref, one, 1)
        gate_ref[rows, :] = gate.astype(jnp.bfloat16)
        new = spread(last_ref, one, 1) * added
        state = new if state is None else spread(keep_ref, one, 1) * state + new
    for h in range(cols // 128):
        out_ref[h] = state[:, h * 128 : (h + 1) * 128]


def finish_kernel(first, local_ref, gate_ref, far_ref, in_ref, gain_ref, member_ref, *rest):
    mixed_ref, sums_ref, held_ref, sems = rest[-4:]
    tokens, cols = local_ref.shape
    per = cols // 128
    row = lax.broadcasted_iota(jnp.int32, (cols, cols), 0)
    col = lax.broadcasted_iota(jnp.int32, (cols, cols), 1)
    mean = jnp.where(row // 128 == col // 128, 1.0 / 128, 0.0).astype(jnp.bfloat16)
    state = jnp.concatenate([in_ref[h] for h in range(per)], axis=1)
    high = state.astype(jnp.bfloat16)
    low = (state - high.astype(jnp.float32)).astype(jnp.bfloat16)
    right = jnp.concatenate([high, low], axis=0)
    gain = gain_ref[:, first : first + cols]
    copies = []
    for b in range(tokens // SPAN):
        rows = slice(b * SPAN, (b + 1) * SPAN)
        far = far_ref[rows, :]
        remote = dot(jnp.concatenate([far, far], axis=1), right)
        gated = local_ref[rows, :].astype(jnp.float32) + gate_ref[rows, :].astype(jnp.float32) * remote
        squares = dot((gated * gated).astype(jnp.bfloat16), mean)
        held_ref[rows, :] = (gated * lax.rsqrt(squares + 1e-05) * gain).astype(jnp.bfloat16)
        copies.append(
            pltpu.make_async_copy(
                held_ref.at[pl.ds(b * SPAN, SPAN), :],
                mixed_ref.at[pl.ds(b * SPAN, SPAN), pl.ds(first, cols)],
                sems.at[b],
            )
        )
        copies[-1].start()
    sums_ref[...] = dot(member_ref[...], held_ref[...])
    for copy in copies:
        copy.wait()


def after(value, *others):
    return lax.optimization_barrier((value, *others))[0]


def swapped(value, axis, by):
    return lax.ppermute(value, axis, [(i, i ^ by) for i in range(lax.axis_size(axis))])


def on_device(
    mixer_input,
    gate_input,
    input_proj,
    output_proj,
    step_raw,
    decay_rate,
    norm_gain,
    doc_lengths,
    partner,
):
    tokens = mixer_input.shape[1]
    width = mixer_input.shape[2]
    heads = decay_rate.shape[0]
    docs = doc_lengths.shape[1]
    blocks = tokens // SPAN
    count = lax.axis_size("ctx")
    here = lax.axis_index("ctx")
    x, z = mixer_input[0], gate_input[0]
    lengths = doc_lengths[0]
    row = lax.axis_index("dp")
    off = here * tokens
    places = [here == k for k in range(count)]
    firsts = [(row ^ j) * docs for j in range(lax.axis_size("dp"))]
    off, *rest = lax.optimization_barrier((off, *places, *firsts))
    places, firsts = rest[:count], rest[count:]
    off = off.astype(jnp.int32).reshape(1)
    per = heads // CHUNKS
    rounds = CHUNKS + DELAY * (count - 2)
    cols = per * 128
    f32, bf16 = jnp.float32, jnp.bfloat16
    smem = pl.BlockSpec(memory_space=pltpu.SMEM)
    whole = lambda *shape: pl.BlockSpec(shape, lambda *i: (0,) * len(shape))
    array = jax.ShapeDtypeStruct
    VM = pl.BlockSpec(memory_space=pltpu.VMEM)
    limit = pltpu.CompilerParams(vmem_limit_bytes=VMEM)

    shapes = [
        array((tokens, heads), f32),
        array((tokens, heads), f32),
        array((blocks, heads), f32),
        array((blocks, heads), f32),
        array((blocks, heads), f32),
        array((rounds * per, 128), f32),
        array((tokens, SPAN + 256), bf16),
        array((blocks * 128, SPAN), bf16),
        array((tokens, 128), bf16),
        array((docs, tokens), bf16),
    ]
    e, f, last, keep, before, rates, left, tails, far, member = pl.pallas_call(
        prepare_kernel,
        grid=(1,),
        in_specs=[smem, smem, whole(tokens, 128), whole(tokens, 128), whole(heads, tokens), whole(1, heads)],
        out_specs=[whole(*s.shape) for s in shapes],
        scratch_shapes=[pltpu.VMEM((heads, 128), f32)],
        out_shape=shapes,
        compiler_params=limit,
        cost_estimate=pl.CostEstimate(flops=1 << 36, bytes_accessed=4 << 20, transcendentals=0),
        name="prepare",
    )(doc_lengths, off, input_proj[0], output_proj[0], step_raw[0], decay_rate.reshape(1, heads))

    def local(c, last):
        return pl.pallas_call(
            functools.partial(local_kernel, c * cols),
            in_specs=[VM] * 9,
            out_specs=[VM] * 3,
            out_shape=[array((tokens, cols), f32), array((tokens, cols), bf16), array((per, 128, 128), f32)],
            compiler_params=limit,
            cost_estimate=pl.CostEstimate(flops=1 << 20, bytes_accessed=1 << 16, transcendentals=0),
            name=f"local{c}",
        )(x, z, e, f, left, tails, last, keep, before)

    def finish(c, incoming, mixed):
        operands = [locals_[c], gates[c], far, incoming, norm_gain.reshape(1, width), member]
        specs = [VM] * len(operands)
        aliases = {}
        if mixed is not None:
            aliases = {len(operands): 0}
            operands.append(mixed)
            specs.append(pl.BlockSpec(memory_space=pl.ANY))
        return pl.pallas_call(
            functools.partial(finish_kernel, c * cols),
            in_specs=specs,
            out_specs=[pl.BlockSpec(memory_space=pl.ANY), VM],
            out_shape=[array((tokens, width), bf16), array((docs, cols), f32)],
            scratch_shapes=[pltpu.VMEM((tokens, cols), bf16), pltpu.SemaphoreType.DMA((blocks,))],
            input_output_aliases=aliases,
            compiler_params=limit,
            cost_estimate=pl.CostEstimate(flops=1 << 20, bytes_accessed=1 << 16, transcendentals=0),
            name=f"finish{c}",
        )(*operands)

    pairs = [(i, (i + 1) % count) for i in range(count)]
    locals_, gates, states, got, sums = [], [], [], [], []
    mixed = None
    sent = None

    def arrived(c, *ready):
        found = [got[c + DELAY * k] for k in range(count - 1)]
        found = lax.optimization_barrier((*found, *ready))
        value = jnp.zeros((per, 128, 128), f32)
        for k in range(1, count):
            value = jnp.where(places[k], found[k - 1], value)
        return value

    for r in range(rounds):
        ready = [] if sent is None else [sent]
        if r < CHUNKS:
            part, gate, state = local(r, after(last, *ready))
            locals_.append(part)
            gates.append(gate)
            states.append(state)
            ready.append(state)
        old = r - 1 - DELAY - DELAY * (count - 2)
        if old >= 0:
            mixed, part = finish(old, arrived(old, sent), mixed)
            sums.append(part)
            ready.append(part)
        mine = states[min(r, CHUNKS - 1)]
        for k in range(1, count):
            c = r - DELAY * k
            if 0 <= c < CHUNKS:
                mine = jnp.where(places[k], states[c], mine)
        if r >= DELAY:
            arriving = after(got[r - DELAY], *ready)
            mine = mine + rates[r * per : (r + 1) * per, None] * jnp.where(places[0], 0.0, arriving)
        elif r > 0:
            mine = after(mine, *ready)
        sent = mine
        got.append(lax.ppermute(sent, "ctx", pairs))
    spread = lengths[:, None].astype(f32)
    pooled, found = [], []

    def gather(low, high):
        totals = jnp.concatenate(sums[low:high], axis=1)
        if count <= 4:
            parts = [swapped(totals, "ctx", j) for j in range(1, count)]
            for part in parts:
                totals = totals + part
        else:
            reach = 1
            while reach < count:
                totals = totals + swapped(totals, "ctx", reach)
                reach *= 2
        mean = totals / spread
        every = [mean] + [swapped(mean, "dp", j) for j in range(1, lax.axis_size("dp"))]
        part = [jnp.dot(mean, one.T, precision=HIGH) for one in every]
        part += [jnp.sum(one * one, axis=1)[None] for one in every]
        pooled.append(mean)
        found.append(jnp.concatenate(part, axis=0))

    low = 0
    for high in BATCHES:
        for c in range(len(sums), high):
            mixed, part = finish(c, arrived(c, *sums[-1:]), mixed)
            sums.append(part)
        gather(low, high)
        low = high
    pooled = jnp.concatenate(pooled, axis=1)
    found = sum(found)
    count_dp = lax.axis_size("dp")
    for j in range(1, lax.axis_size("mp")):
        found = found + swapped(found, "mp", j)
    own = lax.rsqrt(found[count_dp * docs] / WIDTH + 1e-06)
    embedding = pooled * own[:, None]
    total = jnp.zeros((docs,), f32)
    picked = jnp.zeros((docs,), f32)
    ids = jnp.arange(docs, dtype=jnp.int32)
    for j in range(count_dp):
        other = lax.rsqrt(found[count_dp * docs + j] / WIDTH + 1e-06)
        similar = found[j * docs : (j + 1) * docs] * own[:, None] * other[None, :] / (WIDTH * 0.05)
        theirs = firsts[j] + ids
        others = theirs[None, :] != (firsts[0] + ids)[:, None]
        total = total + jnp.sum(jnp.where(others, jnp.exp(similar), 0.0), axis=1)
        picked = picked + jnp.sum(jnp.where(theirs[None, :] == partner[:, None], similar, 0.0), axis=1)
    doc_loss = jnp.log(total) - picked
    return (mixed[None], embedding, doc_loss)


def solution(mesh):
    in_specs = (
        P(("groups", "dp"), "ctx", "mp"),
        P(("groups", "dp"), "ctx", "mp"),
        P(("groups", "dp"), "ctx", None),
        P(("groups", "dp"), "ctx", None),
        P(("groups", "dp"), "mp", "ctx"),
        P("mp"),
        P("mp"),
        P(("groups", "dp"), None),
        P(("groups", "dp")),
    )
    out_specs = (P(("groups", "dp"), "ctx", "mp"), P(("groups", "dp"), "mp"), P(("groups", "dp")))
    return jax.shard_map(
        on_device, mesh=mesh, in_specs=in_specs, out_specs=out_specs, check_vma=False
    )
```

```python
import functools

import jax
import jax.numpy as jnp
from jax import lax
from jax.experimental import pallas as pl
from jax.experimental.pallas import tpu as pltpu
from jax.sharding import PartitionSpec as P

SPAN = 256
WIDTH = 4096
HIGH = lax.Precision.HIGHEST

CHUNKS = 8
DELAY = 3
VMEM = 8 << 20
BATCHES = (CHUNKS,)


def dot(a, b, dims=((1,), (0,))):
    return lax.dot_general(a, b, (dims, ((), ())), preferred_element_type=jnp.float32)


def split3(v):
    hi = v.astype(jnp.bfloat16)
    rest = v - hi.astype(jnp.float32)
    mid = rest.astype(jnp.bfloat16)
    low = (rest - mid.astype(jnp.float32)).astype(jnp.bfloat16)
    return hi, mid, low


def first_end_from(ends, place):
    found = jnp.int32(1 << 30)
    for end in reversed(ends):
        found = jnp.where(end >= place, end, found)
    return found


def last_end_until(ends, place):
    found = jnp.int32(0)
    for end in ends:
        found = jnp.where(end <= place, end, found)
    return found


def decay_kernel(raw_ref, rate_ref, e_ref, f_ref, last_ref, before_ref, total_ref):
    tokens, heads = e_ref.shape
    raw = raw_ref[...]
    steps = (jnp.maximum(raw, 0.0) + jnp.log1p(jnp.exp(-jnp.abs(raw)))).T
    logdecay = -rate_ref[...] * steps
    row = lax.broadcasted_iota(jnp.int32, (SPAN, SPAN), 0)
    col = lax.broadcasted_iota(jnp.int32, (SPAN, SPAN), 1)
    lower = jnp.where(row >= col, 1.0, 0.0).astype(jnp.bfloat16)
    so_far = jnp.zeros((1, heads), jnp.float32)
    for b in range(tokens // SPAN):
        rows = slice(b * SPAN, (b + 1) * SPAN)
        parts = split3(logdecay[rows])
        cum = dot(lower, parts[0]) + (dot(lower, parts[1]) + dot(lower, parts[2]))
        e_ref[rows, :] = jnp.exp(cum)
        f_ref[rows, :] = steps[rows] * jnp.exp(-cum)
        whole = cum[SPAN - 1 :]
        before_ref[b : b + 1, :] = jnp.exp(so_far)
        so_far = so_far + whole
        last_ref[b : b + 1, :] = jnp.exp(whole)
    total_ref[...] = jnp.exp(so_far)


def mask_kernel(
    lengths_ref,
    off_ref,
    b_ref,
    c_ref,
    last_ref,
    total_ref,
    keep_ref,
    rates_ref,
    left_ref,
    tail_ref,
    far_ref,
    member_ref,
    decay_ref,
):
    docs, tokens = member_ref.shape
    heads = last_ref.shape[1]
    off = off_ref[0]
    ends = [lengths_ref[0, 0]]
    for k in range(1, docs):
        ends.append(ends[-1] + lengths_ref[0, k])
    row = lax.broadcasted_iota(jnp.int32, (SPAN, SPAN), 0)
    col = lax.broadcasted_iota(jnp.int32, (SPAN, SPAN), 1)
    places = lax.broadcasted_iota(jnp.int32, (1, tokens), 1) + off
    dend = jnp.full((1, tokens), 1 << 30, jnp.int32)
    docid = jnp.zeros((1, tokens), jnp.int32)
    for k in range(docs - 1, -1, -1):
        dend = jnp.where(ends[k] > places, ends[k], dend)
        docid = docid + (places >= ends[k]).astype(jnp.int32)
    member_ref[...] = (
        (docid == lax.broadcasted_iota(jnp.int32, (docs, tokens), 0)).astype(jnp.float32).astype(jnp.bfloat16)
    )
    device_end = jnp.where(off > 0, first_end_from(ends, off), 0)
    for b in range(tokens // SPAN):
        rows = slice(b * SPAN, (b + 1) * SPAN)
        start = off + b * SPAN
        last_start = last_end_until(ends, start + SPAN - 1)
        prior_end = jnp.where(start > 0, first_end_from(ends, start), 0)
        keep_ref[b : b + 1, :] = last_ref[b : b + 1, :] * jnp.where(last_start < start, 1.0, 0.0)
        bb, cc = b_ref[rows, :], c_ref[rows, :]
        same = (row >= col) & (row + start < dend[:, rows])
        left_ref[rows, 0:SPAN] = jnp.where(same, dot(cc, bb, ((1,), (1,))), 0.0).astype(jnp.bfloat16)
        place = lax.broadcasted_iota(jnp.int32, (SPAN, 128), 0) + start
        cf = cc.astype(jnp.float32)
        reach = jnp.where(place < prior_end, cf, 0.0).astype(jnp.bfloat16)
        left_ref[rows, SPAN : SPAN + 128] = reach
        left_ref[rows, SPAN + 128 :] = reach
        far_ref[rows, :] = jnp.where(place < device_end, cf, 0.0).astype(jnp.bfloat16)
        masked = jnp.where(place >= last_start, bb.astype(jnp.float32), 0.0)
        tail_ref[b * 128 : (b + 1) * 128, :] = masked.T.astype(jnp.bfloat16)
    through = jnp.where(last_end_until(ends, off + tokens - 1) < off, 1.0, 0.0)
    decay_ref[...] = jnp.broadcast_to(total_ref[...] * through, (128, heads)).T
    here = off // tokens
    per = heads // CHUNKS
    for r in range(rates_ref.shape[0] // per):
        chunk = jnp.clip(r - DELAY * here, 0, CHUNKS - 1)
        for h in range(per):
            rates_ref[r * per + h : r * per + h + 1, :] = decay_ref[pl.ds(chunk * per + h, 1), :]


def local_kernel(
    first,
    x_ref,
    z_ref,
    e_ref,
    f_ref,
    left_ref,
    tail_ref,
    last_ref,
    keep_ref,
    before_ref,
    local_ref,
    gate_ref,
    out_ref,
):
    tokens, cols = local_ref.shape
    heads = range(first // 128, (first + cols) // 128)
    lanes = pl.ds(first, cols)

    def spread(ref, rows, count):
        return jnp.concatenate([jnp.broadcast_to(ref[rows, h : h + 1], (count, 128)) for h in heads], axis=1)

    state = None
    for b in range(tokens // SPAN):
        rows = slice(b * SPAN, (b + 1) * SPAN)
        one = slice(b, b + 1)
        scaled = (x_ref[rows, lanes].astype(jnp.float32) * spread(f_ref, rows, SPAN)).astype(jnp.bfloat16)
        added = dot(tail_ref[b * 128 : (b + 1) * 128, :], scaled)
        inner = dot(left_ref[rows, 0:SPAN], scaled)
        if state is not None:
            high = state.astype(jnp.bfloat16)
            low = (state - high.astype(jnp.float32)).astype(jnp.bfloat16)
            inner = inner + dot(left_ref[rows, SPAN:], jnp.concatenate([high, low], axis=0))
        half = 0.5 * z_ref[rows, lanes].astype(jnp.float32)
        gate = (half + half * jnp.tanh(half)) * spread(e_ref, rows, SPAN)
        local_ref[rows, :] = inner * gate
        if b > 0:
            gate = gate * spread(before_ref, one, 1)
        gate_ref[rows, :] = gate.astype(jnp.bfloat16)
        new = spread(last_ref, one, 1) * added
        state = new if state is None else spread(keep_ref, one, 1) * state + new
    for h in range(cols // 128):
        out_ref[h] = state[:, h * 128 : (h + 1) * 128]


def finish_kernel(first, local_ref, gate_ref, far_ref, in_ref, gain_ref, member_ref, *rest):
    mixed_ref, sums_ref, held_ref, sems = rest[-4:]
    tokens, cols = local_ref.shape
    per = cols // 128
    row = lax.broadcasted_iota(jnp.int32, (cols, cols), 0)
    col = lax.broadcasted_iota(jnp.int32, (cols, cols), 1)
    mean = jnp.where(row // 128 == col // 128, 1.0 / 128, 0.0).astype(jnp.bfloat16)
    state = jnp.concatenate([in_ref[h] for h in range(per)], axis=1)
    high = state.astype(jnp.bfloat16)
    low = (state - high.astype(jnp.float32)).astype(jnp.bfloat16)
    right = jnp.concatenate([high, low], axis=0)
    gain = gain_ref[:, first : first + cols]
    copies = []
    for b in range(tokens // SPAN):
        rows = slice(b * SPAN, (b + 1) * SPAN)
        far = far_ref[rows, :]
        remote = dot(jnp.concatenate([far, far], axis=1), right)
        gated = local_ref[rows, :].astype(jnp.float32) + gate_ref[rows, :].astype(jnp.float32) * remote
        squares = dot((gated * gated).astype(jnp.bfloat16), mean)
        held_ref[rows, :] = (gated * lax.rsqrt(squares + 1e-05) * gain).astype(jnp.bfloat16)
        copies.append(
            pltpu.make_async_copy(
                held_ref.at[pl.ds(b * SPAN, SPAN), :],
                mixed_ref.at[pl.ds(b * SPAN, SPAN), pl.ds(first, cols)],
                sems.at[b],
            )
        )
        copies[-1].start()
    sums_ref[...] = dot(member_ref[...], held_ref[...])
    for copy in copies:
        copy.wait()


def after(value, *others):
    return lax.optimization_barrier((value, *others))[0]


def swapped(value, axis, by):
    return lax.ppermute(value, axis, [(i, i ^ by) for i in range(lax.axis_size(axis))])


def on_device(
    mixer_input,
    gate_input,
    input_proj,
    output_proj,
    step_raw,
    decay_rate,
    norm_gain,
    doc_lengths,
    partner,
):
    tokens = mixer_input.shape[1]
    width = mixer_input.shape[2]
    heads = decay_rate.shape[0]
    docs = doc_lengths.shape[1]
    blocks = tokens // SPAN
    count = lax.axis_size("ctx")
    here = lax.axis_index("ctx")
    x, z = mixer_input[0], gate_input[0]
    lengths = doc_lengths[0]
    row = lax.axis_index("dp")
    off = here * tokens
    places = [here == k for k in range(count)]
    firsts = [(row ^ j) * docs for j in range(lax.axis_size("dp"))]
    off, *rest = lax.optimization_barrier((off, *places, *firsts))
    places, firsts = rest[:count], rest[count:]
    off = off.astype(jnp.int32).reshape(1)
    per = heads // CHUNKS
    rounds = CHUNKS + DELAY * (count - 2)
    cols = per * 128
    f32, bf16 = jnp.float32, jnp.bfloat16
    smem = pl.BlockSpec(memory_space=pltpu.SMEM)
    array = jax.ShapeDtypeStruct
    VM = pl.BlockSpec(memory_space=pltpu.VMEM)
    limit = pltpu.CompilerParams(vmem_limit_bytes=VMEM)

    cost = pl.CostEstimate(flops=1 << 36, bytes_accessed=4 << 20, transcendentals=0)
    e, f, last, before, decay = pl.pallas_call(
        decay_kernel,
        in_specs=[VM] * 2,
        out_specs=[VM] * 5,
        out_shape=[array((tokens, heads), f32)] * 2 + [array((blocks, heads), f32)] * 2 + [array((1, heads), f32)],
        compiler_params=limit,
        cost_estimate=cost,
        name="decays",
    )(step_raw[0], decay_rate.reshape(1, heads))
    keep, rates, left, tails, far, member = pl.pallas_call(
        mask_kernel,
        in_specs=[smem, smem] + [VM] * 4,
        out_specs=[VM] * 6,
        out_shape=[
            array((blocks, heads), f32),
            array((rounds * per, 128), f32),
            array((tokens, SPAN + 256), bf16),
            array((blocks * 128, SPAN), bf16),
            array((tokens, 128), bf16),
            array((docs, tokens), bf16),
        ],
        scratch_shapes=[pltpu.VMEM((heads, 128), f32)],
        compiler_params=limit,
        cost_estimate=cost,
        name="masks",
    )(doc_lengths, off, input_proj[0], output_proj[0], last, decay)

    def local(c, last):
        return pl.pallas_call(
            functools.partial(local_kernel, c * cols),
            in_specs=[VM] * 9,
            out_specs=[VM] * 3,
            out_shape=[array((tokens, cols), f32), array((tokens, cols), bf16), array((per, 128, 128), f32)],
            compiler_params=limit,
            cost_estimate=pl.CostEstimate(flops=1 << 20, bytes_accessed=1 << 16, transcendentals=0),
            name=f"local{c}",
        )(x, z, e, f, left, tails, last, keep, before)

    def finish(c, incoming, mixed):
        operands = [locals_[c], gates[c], far, incoming, norm_gain.reshape(1, width), member]
        specs = [VM] * len(operands)
        aliases = {}
        if mixed is not None:
            aliases = {len(operands): 0}
            operands.append(mixed)
            specs.append(pl.BlockSpec(memory_space=pl.ANY))
        return pl.pallas_call(
            functools.partial(finish_kernel, c * cols),
            in_specs=specs,
            out_specs=[pl.BlockSpec(memory_space=pl.ANY), VM],
            out_shape=[array((tokens, width), bf16), array((docs, cols), f32)],
            scratch_shapes=[pltpu.VMEM((tokens, cols), bf16), pltpu.SemaphoreType.DMA((blocks,))],
            input_output_aliases=aliases,
            compiler_params=limit,
            cost_estimate=pl.CostEstimate(flops=1 << 20, bytes_accessed=1 << 16, transcendentals=0),
            name=f"finish{c}",
        )(*operands)

    pairs = [(i, (i + 1) % count) for i in range(count)]
    locals_, gates, states, got, sums = [], [], [], [], []
    mixed = None
    sent = None

    def arrived(c, *ready):
        found = [got[c + DELAY * k] for k in range(count - 1)]
        found = lax.optimization_barrier((*found, *ready))
        value = jnp.zeros((per, 128, 128), f32)
        for k in range(1, count):
            value = jnp.where(places[k], found[k - 1], value)
        return value

    for r in range(rounds):
        ready = [] if sent is None else [sent]
        if r < CHUNKS:
            part, gate, state = local(r, after(last, *ready))
            locals_.append(part)
            gates.append(gate)
            states.append(state)
            ready.append(state)
        old = r - 1 - DELAY - DELAY * (count - 2)
        if old >= 0:
            mixed, part = finish(old, arrived(old, sent), mixed)
            sums.append(part)
            ready.append(part)
        mine = states[min(r, CHUNKS - 1)]
        for k in range(1, count):
            c = r - DELAY * k
            if 0 <= c < CHUNKS:
                mine = jnp.where(places[k], states[c], mine)
        if r >= DELAY:
            arriving = after(got[r - DELAY], *ready)
            mine = mine + rates[r * per : (r + 1) * per, None] * jnp.where(places[0], 0.0, arriving)
        elif r > 0:
            mine = after(mine, *ready)
        sent = mine
        got.append(lax.ppermute(sent, "ctx", pairs))
    spread = lengths[:, None].astype(f32)
    pooled, found = [], []

    def gather(low, high):
        totals = jnp.concatenate(sums[low:high], axis=1)
        reach = 1
        while reach < count:
            totals = totals + swapped(totals, "ctx", reach)
            reach *= 2
        mean = totals / spread
        every = [mean] + [swapped(mean, "dp", j) for j in range(1, lax.axis_size("dp"))]
        part = [jnp.dot(mean, one.T, precision=HIGH) for one in every]
        part += [jnp.sum(one * one, axis=1)[None] for one in every]
        pooled.append(mean)
        found.append(jnp.concatenate(part, axis=0))

    low = 0
    for high in BATCHES:
        for c in range(len(sums), high):
            mixed, part = finish(c, arrived(c, sent, *sums[-1:]), mixed)
            sums.append(part)
        gather(low, high)
        low = high
    pooled = jnp.concatenate(pooled, axis=1)
    found = sum(found)
    count_dp = lax.axis_size("dp")
    for j in range(1, lax.axis_size("mp")):
        found = found + swapped(found, "mp", j)
    own = lax.rsqrt(found[count_dp * docs] / WIDTH + 1e-06)
    embedding = pooled * own[:, None]
    total = jnp.zeros((docs,), f32)
    picked = jnp.zeros((docs,), f32)
    ids = jnp.arange(docs, dtype=jnp.int32)
    for j in range(count_dp):
        other = lax.rsqrt(found[count_dp * docs + j] / WIDTH + 1e-06)
        similar = found[j * docs : (j + 1) * docs] * own[:, None] * other[None, :] / (WIDTH * 0.05)
        theirs = firsts[j] + ids
        others = theirs[None, :] != (firsts[0] + ids)[:, None]
        total = total + jnp.sum(jnp.where(others, jnp.exp(similar), 0.0), axis=1)
        picked = picked + jnp.sum(jnp.where(theirs[None, :] == partner[:, None], similar, 0.0), axis=1)
    doc_loss = jnp.log(total) - picked
    return (mixed[None], embedding, doc_loss)


def solution(mesh):
    in_specs = (
        P(("groups", "dp"), "ctx", "mp"),
        P(("groups", "dp"), "ctx", "mp"),
        P(("groups", "dp"), "ctx", None),
        P(("groups", "dp"), "ctx", None),
        P(("groups", "dp"), "mp", "ctx"),
        P("mp"),
        P("mp"),
        P(("groups", "dp"), None),
        P(("groups", "dp")),
    )
    out_specs = (P(("groups", "dp"), "ctx", "mp"), P(("groups", "dp"), "mp"), P(("groups", "dp")))
    return jax.shard_map(
        on_device, mesh=mesh, in_specs=in_specs, out_specs=out_specs, check_vma=False
    )
```
